32 devices in a mesh: ctx: 8 (over z, y), tp: 4 (over x, core).
Axes of the slice: x: 2, y: 2, z: 4, core: 2. Of those that a mesh axis runs over, the one named last changes fastest.
Arguments:
- query_proj: bfloat16 [2048, 8192], P('ctx', 'tp'), may hold values from -24 to 24, as said below
- key_proj: bfloat16 [2048, 8192], P('ctx', 'tp'), may hold values from -6 to 6
- value_proj: bfloat16 [2048, 8192], P('ctx', 'tp'), may hold values from -6 to 6
- filters: bfloat16 [128, 8192], P(None, 'tp'), may hold values from -6 to 6, as said below
- norm_gain: float32 [8192], P('tp'), may hold values from 0.1 to 1.9
- grad_out: bfloat16 [2048, 8192], P('ctx', 'tp'), may hold values from -6 to 6
Outputs:
- mixed: bfloat16 [2048, 8192], P('ctx', 'tp')
- grad_query: bfloat16 [2048, 8192], P('ctx', 'tp')
- grad_key: bfloat16 [2048, 8192], P('ctx', 'tp')
- grad_value: bfloat16 [2048, 8192], P('ctx', 'tp')
- grad_filter: float32 [128, 8192], P(None, 'tp')
- grad_gain: float32 [8192], P('tp')
The draws below stay inside these ranges and needn't reach their ends.
Inputs may be any that keep to these rules, and one draw needn't show every extreme that they name: `query_proj`: finite real values. `filters`: finite real values.
All inputs are finite; a program needn't handle non-finite values.
Results may differ from the reference program's by a relative error of at most 0.0051.
Values may be sent and summed in bfloat16 or wider, within the bound.
A program may use at most 64 MiB of HBM per device.

```python
import math
import jax
import jax.numpy as jnp
from jax import lax

D = 8192
TAPS = 128
TOKENS = 2048


def draw_query_proj(key, part):
    channel = jnp.arange(D, dtype=jnp.float32)
    col_scale = jnp.exp(jnp.log(3.0) * channel / (D - 1))
    base = jnp.clip(jax.random.normal(key, (TOKENS, D), jnp.float32), -6.0, 6.0)
    return (base * col_scale[None, :]).astype(jnp.bfloat16)


def draw_filters(key, part):
    rate_key = jax.random.fold_in(key, 11)
    tap_key = jax.random.fold_in(key, 12)
    low, high = (0.5 / TAPS, 30.0 / TAPS)
    rates = jnp.exp(jax.random.uniform(rate_key, (D,), jnp.float32, jnp.log(low), jnp.log(high)))
    steps = jnp.arange(TAPS, dtype=jnp.float32)[:, None]
    energy = (1.0 - jnp.exp(-2.0 * rates * TAPS)) / (1.0 - jnp.exp(-2.0 * rates))
    base = jnp.clip(jax.random.normal(tap_key, (TAPS, D), jnp.float32), -6.0, 6.0)
    taps_out = base * jnp.exp(-rates[None, :] * steps) / jnp.sqrt(energy)[None, :]
    return jnp.clip(taps_out, -6.0, 6.0).astype(jnp.bfloat16)


def block_levels(stream_key, dims, cuts, least, largest):
    factor_of, own = 1.0, jax.random.fold_in(stream_key, 6)
    for position, blocks in cuts:
        steps = jnp.exp(jax.random.uniform(jax.random.fold_in(own, position), (blocks,), jnp.float32, least / len(cuts), largest / len(cuts)))
        factor_of = factor_of * jnp.repeat(steps, dims[position] // blocks).reshape([-1 if axis == position else 1 for axis in range(len(dims))])
    return factor_of


def bell_draw(key, dims, scale, most, split=(), kind=jnp.bfloat16):
    drawn = scale * jax.random.normal(key, dims, jnp.float32)
    if split:
        drawn = drawn * block_levels(key, dims, split, -0.22, 0.18)
    return jnp.clip(drawn, -most, most).astype(kind)


def setup_inputs(seed: int = 0) -> dict:
    key_of = jax.random.split(jax.random.key(seed), 7)
    return {
        "query_proj": draw_query_proj(jax.random.fold_in(key_of[6], 71), 0),
        "key_proj": bell_draw(key_of[1], (TOKENS, D), 1.0, 6.0, ((0, 8), (1, 4))),
        "value_proj": bell_draw(key_of[2], (TOKENS, D), 1.0, 6.0, ((0, 8), (1, 4))),
        "filters": draw_filters(jax.random.fold_in(key_of[6], 71), 0),
        "norm_gain": jnp.clip(1.0 + 0.18 * jax.random.normal(key_of[4], (D,), jnp.float32), 0.1, 1.9),
        "grad_out": bell_draw(key_of[5], (TOKENS, D), 1.0, 6.0, ((0, 8), (1, 4))),
    }


EPS = 1e-06

def causal_taps(signal, weights):
    length = signal.shape[0]
    padded = jnp.concatenate([jnp.zeros((TAPS - 1, signal.shape[1]), signal.dtype), signal], 0)

    def add_tap(tap_index, running):
        tap_index = jnp.asarray(tap_index).astype(jnp.int32)
        first_row = (TAPS - 1 - tap_index).astype(jnp.int32)
        return running + weights[tap_index] * lax.dynamic_slice_in_dim(padded, first_row, length, 0)
    return lax.fori_loop(0, TAPS, add_tap, jnp.zeros_like(signal))

def later_taps(signal, weights):
    length = signal.shape[0]
    padded = jnp.concatenate([signal, jnp.zeros((TAPS - 1, signal.shape[1]), signal.dtype)], 0)

    def add_tap(tap_index, running):
        tap_index = jnp.asarray(tap_index).astype(jnp.int32)
        return running + weights[tap_index] * lax.dynamic_slice_in_dim(padded, tap_index, length, 0)
    return lax.fori_loop(0, TAPS, add_tap, jnp.zeros_like(signal))

def filter_terms(grad_conv, key_value):
    length = grad_conv.shape[0]
    padded = jnp.concatenate([jnp.zeros((TAPS - 1, key_value.shape[1]), key_value.dtype), key_value], 0)

    def one_tap(tap_index):
        first_row = (TAPS - 1 - tap_index).astype(jnp.int32)
        return lax.optimization_barrier(jnp.sum(grad_conv * lax.dynamic_slice_in_dim(padded, first_row, length, 0), 0))
    return lax.map(one_tap, jnp.arange(TAPS, dtype=jnp.int32))

def reference(query_proj, key_proj, value_proj, filters, norm_gain, grad_out):
    total_rows = query_proj.shape[0]
    block_cols = math.gcd(D, 256)
    block_count = D // block_cols
    filt_wide = filters.astype(jnp.float32)

    def cols(array, block_index):
        return lax.dynamic_slice_in_dim(array, (block_index * block_cols).astype(jnp.int32), block_cols, array.ndim - 1)

    def forward_block(block_index):
        key_value = (cols(key_proj, block_index).astype(jnp.float32) * cols(value_proj, block_index).astype(jnp.float32)).astype(jnp.bfloat16)
        conv_out = causal_taps(key_value.astype(jnp.float32), cols(filt_wide, block_index))
        return (key_value, conv_out)
    indices = jnp.arange(block_count, dtype=jnp.int32)
    kv_blocks, conv_blocks = lax.map(forward_block, indices)

    def squares_block(block_index):
        gated = cols(query_proj, block_index).astype(jnp.float32) * conv_blocks[block_index]
        return lax.optimization_barrier(jnp.sum(gated * gated, 1))
    row_sq = lax.optimization_barrier(jnp.sum(lax.map(squares_block, indices), 0))
    row_rms = jnp.sqrt(row_sq / D + EPS)

    def mean_block(block_index):
        gated = cols(query_proj, block_index).astype(jnp.float32) * conv_blocks[block_index]
        normed = gated / row_rms[:, None]
        grad_scaled = cols(grad_out, block_index).astype(jnp.float32) * cols(norm_gain, block_index)
        return lax.optimization_barrier(jnp.sum(grad_scaled * normed, 1))
    row_mean = lax.optimization_barrier(jnp.sum(lax.map(mean_block, indices), 0)) / D
    scale = 1.0 / math.sqrt(total_rows)

    def backward_block(block_index):
        query_b = cols(query_proj, block_index).astype(jnp.float32)
        conv_out = conv_blocks[block_index]
        key_value = kv_blocks[block_index]
        gain_b = cols(norm_gain, block_index)
        grad_b = cols(grad_out, block_index).astype(jnp.float32)
        gated = query_b * conv_out
        normed = gated / row_rms[:, None]
        mixed = (normed * gain_b).astype(jnp.bfloat16)
        grad_scaled = grad_b * gain_b
        grad_gated = (grad_scaled - normed * row_mean[:, None]) / row_rms[:, None]
        grad_query = (grad_gated * conv_out).astype(jnp.bfloat16)
        grad_conv = (grad_gated * query_b).astype(jnp.bfloat16)
        grad_kv = later_taps(grad_conv.astype(jnp.float32), cols(filt_wide, block_index))
        grad_key = (grad_kv * cols(value_proj, block_index).astype(jnp.float32)).astype(jnp.bfloat16)
        grad_value = (grad_kv * cols(key_proj, block_index).astype(jnp.float32)).astype(jnp.bfloat16)
        grad_filter = filter_terms(grad_conv.astype(jnp.float32), key_value.astype(jnp.float32)) * scale
        grad_gain = lax.optimization_barrier(jnp.sum(grad_b * normed, 0)) * scale
        return (mixed, grad_query, grad_key, grad_value, grad_filter, grad_gain)
    outs = lax.map(backward_block, indices)

    def join(stacked):
        return jnp.transpose(stacked, (1, 0, 2)).reshape(stacked.shape[1], D)
    return (join(outs[0]), join(outs[1]), join(outs[2]), join(outs[3]), join(outs[4]), outs[5].reshape(D))
```

```python
import math

import jax
import jax.numpy as jnp
import numpy as np
from jax import lax
from jax.sharding import PartitionSpec as P

EPS = 1e-06
F32 = jnp.float32
BF16 = jnp.bfloat16


def passed_along(array, axis, by):
    length = lax.axis_size(axis)
    pairs = [(i, i + by) for i in range(length) if 0 <= i + by < length]
    return lax.ppermute(array, axis, pairs)


def split(array):
    high = array.astype(BF16)
    return high, (array - high.astype(array.dtype)).astype(BF16)


def dft_matrices(block):
    length = 2 * block
    freq = np.concatenate([np.arange(0, block, 2), np.arange(1, block, 2)])
    at = np.arange(block)
    angle = 2.0 * np.pi * ((freq[:, None] * at[None, :]) % length) / length
    sign = np.where(at % 2 == 0, 1.0, -1.0)
    real, imag = np.cos(angle), -np.sin(angle)
    imag[0] = sign
    forward = np.concatenate([real, imag], 0)
    back = np.concatenate([2.0 * real, 2.0 * imag], 0)
    back[0] *= 0.5
    back[block] *= 0.5
    back = back.T / length

    def parts(matrix):
        matrix = matrix.astype(np.float32)
        high = matrix.astype(jnp.bfloat16)
        low = (matrix - high.astype(np.float32)).astype(jnp.bfloat16)
        return high, low

    fh, fl = parts(forward)
    bh, bl = parts(back)
    return np.concatenate([fh, fl], 1), np.concatenate([bh, bl, bh], 1)


def flip(spec):
    quarter = spec.shape[0] // 4
    return jnp.concatenate(
        [spec[:quarter], -spec[quarter : 2 * quarter], spec[2 * quarter : 3 * quarter], -spec[3 * quarter :]], 0
    )


def product(a, b, conj):
    half = a.shape[0] // 2
    ar, ai, br, bi = a[:half], a[half:], b[:half], b[half:]
    first = lax.broadcasted_iota(jnp.int32, ar.shape, 0) == 0
    rr, ii = ar * br, ai * bi
    if conj:
        real = jnp.where(first, rr, rr + ii)
        imag = jnp.where(first, ii, ai * br - ar * bi)
    else:
        real = jnp.where(first, rr, rr - ii)
        imag = jnp.where(first, ii, ai * br + ar * bi)
    return jnp.concatenate([real, imag], 0)


def on_device(query_proj, key_proj, value_proj, filters, norm_gain, grad_out):
    row_count, col_count = query_proj.shape
    taps = filters.shape[0]
    blocks = row_count // taps
    width = col_count * lax.axis_size("tp")
    scale = 1.0 / math.sqrt(row_count * lax.axis_size("ctx"))
    forward, back = dft_matrices(taps)

    def to_spec(rows):
        return jnp.dot(forward, jnp.concatenate([rows, rows], 0), preferred_element_type=F32)

    def from_spec(spec):
        high, low = split(spec)
        return jnp.dot(back, jnp.concatenate([high, high, low], 0), preferred_element_type=F32)

    key_wide = key_proj.astype(F32)
    value_wide = value_proj.astype(F32)
    query_wide = query_proj.astype(F32)
    key_value = (key_wide * value_wide).astype(BF16)
    before = passed_along(key_value[row_count - taps :], "ctx", 1)
    filt = to_spec(filters)
    kv_spec = [to_spec(before)] + [to_spec(key_value[b * taps : (b + 1) * taps]) for b in range(blocks)]
    kv_win = [kv_spec[b + 1] + flip(kv_spec[b]) for b in range(blocks)]
    conv_out = jnp.concatenate([from_spec(product(w, filt, False)) for w in kv_win], 0)
    gated = query_wide * conv_out
    grad_wide = grad_out.astype(F32)
    grad_scaled = grad_wide * norm_gain
    stats = lax.psum(jnp.stack([jnp.sum(gated * gated, 1), jnp.sum(grad_scaled * gated, 1)]), "tp")
    inv_rms = lax.rsqrt(stats[0] / width + EPS)
    row_mean = stats[1] * inv_rms / width
    normed = gated * inv_rms[:, None]
    mixed = (normed * norm_gain).astype(BF16)
    grad_gated = (grad_scaled - normed * row_mean[:, None]) * inv_rms[:, None]
    grad_query = (grad_gated * conv_out).astype(BF16)
    grad_conv = (grad_gated * query_wide).astype(BF16)
    after = passed_along(grad_conv[:taps], "ctx", -1)
    gc_spec = [to_spec(grad_conv[b * taps : (b + 1) * taps]) for b in range(blocks)]
    filter_spec = sum(product(gc_spec[b], kv_win[b], True) for b in range(blocks))
    filter_local = from_spec(filter_spec)
    gain_local = jnp.sum(grad_wide * normed, 0)
    total = lax.psum(jnp.concatenate([filter_local, gain_local[None]], 0), "ctx") * scale
    gc_spec = gc_spec + [to_spec(after)]
    gc_win = [gc_spec[b] + flip(gc_spec[b + 1]) for b in range(blocks)]
    grad_kv = jnp.concatenate([from_spec(product(w, filt, True)) for w in gc_win], 0)
    grad_key = (grad_kv * value_wide).astype(BF16)
    grad_value = (grad_kv * key_wide).astype(BF16)
    return (mixed, grad_query, grad_key, grad_value, total[:taps], total[taps])


def solution(mesh):
    placed = (
        P("ctx", "tp"),
        P("ctx", "tp"),
        P("ctx", "tp"),
        P(None, "tp"),
        P("tp"),
        P("ctx", "tp"),
    )
    return jax.shard_map(
        on_device,
        mesh=mesh,
        in_specs=placed,
        out_specs=(
            P("ctx", "tp"),
            P("ctx", "tp"),
            P("ctx", "tp"),
            P("ctx", "tp"),
            P(None, "tp"),
            P("tp"),
        ),
        check_vma=False,
    )
```

```python
import functools
import math

import jax
import jax.numpy as jnp
import numpy as np
from jax import lax
from jax.experimental import pallas as pl
from jax.experimental.pallas import tpu as pltpu
from jax.sharding import PartitionSpec as P

EPS = 1e-06
F32 = jnp.float32
BF16 = jnp.bfloat16
MESH = pl.DeviceIdType.MESH
STEP = 256


def split(array):
    high = array.astype(BF16)
    return high, (array - high.astype(array.dtype)).astype(BF16)


def dft_matrices(block):
    length = 2 * block
    freq = np.concatenate([np.arange(0, block, 2), np.arange(1, block, 2)])
    at = np.arange(block)
    angle = 2.0 * np.pi * ((freq[:, None] * at[None, :]) % length) / length
    sign = np.where(at % 2 == 0, 1.0, -1.0)
    real, imag = np.cos(angle), -np.sin(angle)
    imag[0] = sign
    forward = np.concatenate([real, imag], 0)
    back = np.concatenate([2.0 * real, 2.0 * imag], 0)
    back[0] *= 0.5
    back[block] *= 0.5
    back = back.T / length

    def parts(matrix):
        matrix = matrix.astype(np.float32)
        high = matrix.astype(jnp.bfloat16)
        low = (matrix - high.astype(np.float32)).astype(jnp.bfloat16)
        return high, low

    fh, fl = parts(forward)
    bh, bl = parts(back)
    return np.concatenate([fh, fl], 1), np.concatenate([bh, bl, bh], 1)


def flip(spec):
    quarter = spec.shape[0] // 4
    return jnp.concatenate(
        [spec[:quarter], -spec[quarter : 2 * quarter], spec[2 * quarter : 3 * quarter], -spec[3 * quarter :]], 0
    )


def product(a, b, conj):
    half = a.shape[0] // 2
    ar, ai, br, bi = a[:half], a[half:], b[:half], b[half:]
    first = lax.broadcasted_iota(jnp.int32, ar.shape, 0) == 0
    rr, ii = ar * br, ai * bi
    if conj:
        real = jnp.where(first, rr, rr + ii)
        imag = jnp.where(first, ii, ai * br - ar * bi)
    else:
        real = jnp.where(first, rr, rr - ii)
        imag = jnp.where(first, ii, ai * br + ar * bi)
    return jnp.concatenate([real, imag], 0)


def kernel(n, t, inside, *refs):
    (q_ref, k_ref, v_ref, f_ref, gain_ref, go_ref, forward_ref, back_ref) = refs[:8]
    (mixed_ref, gq_ref, gk_ref, gv_ref, gf_ref, gg_ref) = refs[8:14]
    (tail, before, head, after, filt, win, gcs, conv, sq, dots, stat, stat_in, fs, rs_in, red, ag_in, gsend, g_in) = refs[14:32]
    (t_send, t_recv, h_send, h_recv, s_send, s_recv, r_send, r_recv, a_send, a_recv, g_send, g_recv) = refs[32:]
    rows, cols = q_ref.shape
    taps = f_ref.shape[0]
    blocks = rows // taps
    steps = cols // STEP
    width = cols * t
    scale = 1.0 / math.sqrt(rows * n)
    me, tp = lax.axis_index("ctx"), lax.axis_index("tp")
    has_prev, has_next = me > 0, me < n - 1

    barrier = pltpu.get_barrier_semaphore()

    def greet(axis, peer):
        pl.semaphore_signal(barrier, inc=1, device_id={axis: peer}, device_id_type=MESH)

    for d in range(1, t):
        greet("tp", lax.rem(tp + d, t))
    pl.when(has_prev)(lambda: greet("ctx", me - 1))
    pl.when(has_next)(lambda: greet("ctx", me + 1))
    if inside:
        for d in range(1, n):
            peer = lax.rem(me + d, n)
            far = jnp.logical_and(peer != me + 1, peer != me - 1)
            pl.when(far)(lambda peer=peer: greet("ctx", peer))
        pl.semaphore_wait(barrier, t - 1 + n - 1)
    else:
        pl.semaphore_wait(barrier, t - 1)
        pl.when(has_prev)(lambda: pl.semaphore_wait(barrier, 1))
        pl.when(has_next)(lambda: pl.semaphore_wait(barrier, 1))

    def remote(src, dst, send, recv, axis, peer):
        return pltpu.make_async_remote_copy(
            src_ref=src, dst_ref=dst, send_sem=send, recv_sem=recv,
            device_id={axis: peer}, device_id_type=MESH,
        )

    def tail_copy(c):
        return remote(tail.at[c], before.at[c], t_send.at[c], t_recv.at[c], "ctx", me + 1)

    def head_copy(c):
        return remote(head.at[c], after.at[c], h_send.at[c], h_recv.at[c], "ctx", me - 1)

    def to_spec(block):
        return jnp.dot(forward_ref[...], jnp.concatenate([block, block], 0), preferred_element_type=F32)

    def from_spec(spec):
        high, low = split(spec)
        return jnp.dot(back_ref[...], jnp.concatenate([high, high, low], 0), preferred_element_type=F32)

    def part(b):
        return pl.ds(b * taps, taps)

    def at(c):
        return pl.ds(pl.multiple_of(c * STEP, STEP), STEP)

    def key_value(b, c):
        return (k_ref[part(b), at(c)].astype(F32) * v_ref[part(b), at(c)].astype(F32)).astype(BF16)

    @pl.loop(0, steps)
    def _(c):
        tail[c] = key_value(blocks - 1, c)
        pl.when(has_next)(lambda: tail_copy(c).start())

    sq[...] = jnp.zeros_like(sq)
    dots[...] = jnp.zeros_like(dots)

    def forward_block(b, c):
        out = from_spec(product(win[c, b], filt[c], False))
        conv[c, part(b)] = out
        gated = q_ref[part(b), at(c)].astype(F32) * out
        graded = go_ref[part(b), at(c)].astype(F32) * gain_ref[:, at(c)] * gated
        square = gated * gated
        for i in range(STEP // 128):
            sq[part(b)] += square[:, i * 128 : (i + 1) * 128]
            dots[part(b)] += graded[:, i * 128 : (i + 1) * 128]

    @pl.loop(0, steps)
    def _(c):
        filt[c] = to_spec(f_ref[:, at(c)])
        spec = to_spec(key_value(0, c))
        win[c, 0] = spec
        for b in range(1, blocks):
            last, spec = spec, to_spec(key_value(b, c))
            win[c, b] = spec + flip(last)
            forward_block(b, c)

    @pl.when(jnp.logical_not(has_prev))
    def _():
        before[...] = jnp.zeros_like(before)

    @pl.loop(0, steps)
    def _(c):
        pl.when(has_prev)(lambda: tail_copy(c).wait_recv())
        win[c, 0] += flip(to_spec(before[c]))
        forward_block(0, c)

    lane = lax.broadcasted_iota(jnp.int32, (rows, 128), 1)
    sums = jnp.where(lane == 0, jnp.sum(sq[...], 1, keepdims=True), jnp.sum(dots[...], 1, keepdims=True))
    stat[...] = sums.T[:8]

    def stat_copy(d):
        return remote(stat, stat_in.at[d - 1], s_send.at[d - 1], s_recv.at[d - 1], "tp", lax.rem(tp + d, t))

    for d in range(1, t):
        stat_copy(d).start()
    total = stat[...]
    for d in range(1, t):
        stat_copy(d).wait_recv()
        total += stat_in[d - 1]
    total = jnp.concatenate([total] * 16, 0).T
    inv_rms = lax.rsqrt(total[:, 0:1] / width + EPS)
    row_mean = total[:, 1:2] * inv_rms / width
    sq[...] = jnp.broadcast_to(inv_rms, sq.shape)
    dots[...] = jnp.broadcast_to(row_mean, dots.shape)

    def backward_block(b, c):
        inv, mean = sq[part(b), 0:1], dots[part(b), 0:1]
        query = q_ref[part(b), at(c)].astype(F32)
        grad = go_ref[part(b), at(c)].astype(F32)
        gain = gain_ref[:, at(c)]
        out = conv[c, part(b)]
        normed = query * out * inv
        mixed_ref[part(b), at(c)] = (normed * gain).astype(BF16)
        gated = (grad * gain - normed * mean) * inv
        gq_ref[part(b), at(c)] = (gated * out).astype(BF16)
        return (gated * query).astype(BF16), jnp.sum(grad * normed, 0, keepdims=True)

    @pl.loop(0, steps)
    def _(c):
        grad_conv, gain_sum = backward_block(0, c)
        head[c] = grad_conv
        pl.when(has_prev)(lambda: head_copy(c).start())
        spec = to_spec(grad_conv)
        gcs[c, 0] = spec
        gf = product(spec, win[c, 0], True)
        for b in range(1, blocks):
            grad_conv, more = backward_block(b, c)
            gain_sum += more
            spec = to_spec(grad_conv)
            gcs[c, b] = spec
            gcs[c, b - 1] += flip(spec)
            gf += product(spec, win[c, b], True)
        gf = from_spec(gf) * scale
        gsend[:, at(c)] = gain_sum * scale
        if inside:
            size = taps // n
            rounded = gf.astype(BF16)
            for r in range(n):
                fs[r, :, at(c)] = rounded[r * size : (r + 1) * size]
        else:
            gf_ref[:, at(c)] = gf

    def rs_copy(d):
        peer = lax.rem(me + d, n)
        return remote(fs.at[peer], rs_in.at[d - 1], r_send.at[d - 1], r_recv.at[d - 1], "ctx", peer)

    def ag_copy(d):
        peer = lax.rem(me + d, n)
        return remote(red, ag_in.at[d - 1], a_send.at[d - 1], a_recv.at[d - 1], "ctx", peer)

    def gain_copy(d):
        peer = lax.rem(me + d, n)
        return remote(gsend, g_in.at[d - 1], g_send.at[d - 1], g_recv.at[d - 1], "ctx", peer)

    if inside:
        for d in range(1, n):
            rs_copy(d).start()
        for d in range(1, n):
            gain_copy(d).start()

    def last_block(b, c):
        grad_kv = from_spec(product(gcs[c, b], filt[c], True))
        gk_ref[part(b), at(c)] = (grad_kv * v_ref[part(b), at(c)].astype(F32)).astype(BF16)
        gv_ref[part(b), at(c)] = (grad_kv * k_ref[part(b), at(c)].astype(F32)).astype(BF16)

    @pl.loop(0, steps)
    def _(c):
        for b in range(blocks - 1):
            last_block(b, c)

    if inside:
        size = taps // n
        for d in range(1, n):
            rs_copy(d).wait_recv()

        @pl.loop(0, steps)
        def _(c):
            whole = fs[me, :, at(c)].astype(F32)
            for d in range(1, n):
                whole += rs_in[d - 1, :, at(c)].astype(F32)
            red[:, at(c)] = whole.astype(BF16)

        for d in range(1, n):
            ag_copy(d).start()

    @pl.when(jnp.logical_not(has_next))
    def _():
        after[...] = jnp.zeros_like(after)

    @pl.loop(0, steps)
    def _(c):
        pl.when(has_next)(lambda: head_copy(c).wait_recv())
        gcs[c, blocks - 1] += flip(to_spec(after[c]))
        last_block(blocks - 1, c)

    if inside:
        gain_sum = gsend[...]
        for d in range(1, n):
            gain_copy(d).wait_recv()
            gain_sum += g_in[d - 1]
        gg_ref[...] = gain_sum
        gf_ref[pl.ds(pl.multiple_of(me * size, size), size)] = red[...].astype(F32)
        for d in range(1, n):
            owner = lax.rem(me + n - d, n)
            ag_copy(d).wait_recv()
            gf_ref[pl.ds(pl.multiple_of(owner * size, size), size)] = ag_in[d - 1].astype(F32)
        for d in range(1, n):
            rs_copy(d).wait_send()
            gain_copy(d).wait_send()
            ag_copy(d).wait_send()
    else:
        gg_ref[...] = gsend[...]
    for d in range(1, t):
        stat_copy(d).wait_send()

    @pl.loop(0, steps)
    def _(c):
        pl.when(has_next)(lambda: tail_copy(c).wait_send())
        pl.when(has_prev)(lambda: head_copy(c).wait_send())


def on_device(query_proj, key_proj, value_proj, filters, norm_gain, grad_out):
    rows, cols = query_proj.shape
    taps = filters.shape[0]
    n, t = lax.axis_size("ctx"), lax.axis_size("tp")
    inside = taps % (16 * n) == 0
    size, peers = (taps // n, n - 1) if inside else (16, 1)
    blocks, steps = rows // taps, cols // STEP
    forward, back = dft_matrices(taps)
    wide = jax.ShapeDtypeStruct((rows, cols), BF16)
    mem = pl.BlockSpec(memory_space=pltpu.VMEM)
    dma = pltpu.SemaphoreType.DMA
    outs = pl.pallas_call(
        functools.partial(kernel, n, t, inside),
        out_shape=(wide, wide, wide, wide,
                   jax.ShapeDtypeStruct((taps, cols), F32), jax.ShapeDtypeStruct((1, cols), F32)),
        in_specs=[mem] * 8,
        out_specs=(mem,) * 6,
        scratch_shapes=[
            pltpu.VMEM((steps, taps, STEP), BF16),
            pltpu.VMEM((steps, taps, STEP), BF16),
            pltpu.VMEM((steps, taps, STEP), BF16),
            pltpu.VMEM((steps, taps, STEP), BF16),
            pltpu.VMEM((steps, 2 * taps, STEP), F32),
            pltpu.VMEM((steps, blocks, 2 * taps, STEP), F32),
            pltpu.VMEM((steps, blocks, 2 * taps, STEP), F32),
            pltpu.VMEM((steps, rows, STEP), F32),
            pltpu.VMEM((rows, 128), F32),
            pltpu.VMEM((rows, 128), F32),
            pltpu.VMEM((8, rows), F32),
            pltpu.VMEM((t - 1, 8, rows), F32),
            pltpu.VMEM((n if inside else 1, size, cols), BF16),
            pltpu.VMEM((peers, size, cols), BF16),
            pltpu.VMEM((size, cols), BF16),
            pltpu.VMEM((peers, size, cols), BF16),
            pltpu.VMEM((1, cols), F32),
            pltpu.VMEM((peers, 1, cols), F32),
        ]
        + [dma((steps,))] * 4 + [dma((t - 1,))] * 2 + [dma((peers,))] * 6,
        compiler_params=pltpu.CompilerParams(
            collective_id=0, has_side_effects=True, vmem_limit_bytes=56 * 1024 * 1024
        ),
        cost_estimate=pl.CostEstimate(flops=4_000_000_000, bytes_accessed=10_000_000, transcendentals=0),
    )(query_proj, key_proj, value_proj, filters, norm_gain[None], grad_out,
      jnp.asarray(forward), jnp.asarray(back))
    mixed, grad_query, grad_key, grad_value, grad_filter, grad_gain = outs
    if not inside:
        grad_filter, grad_gain = lax.psum((grad_filter, grad_gain), "ctx")
    return (mixed, grad_query, grad_key, grad_value, grad_filter, grad_gain[0])


def solution(mesh):
    placed = (
        P("ctx", "tp"),
        P("ctx", "tp"),
        P("ctx", "tp"),
        P(None, "tp"),
        P("tp"),
        P("ctx", "tp"),
    )
    return jax.shard_map(
        on_device,
        mesh=mesh,
        in_specs=placed,
        out_specs=(
            P("ctx", "tp"),
            P("ctx", "tp"),
            P("ctx", "tp"),
            P("ctx", "tp"),
            P(None, "tp"),
            P("tp"),
        ),
        check_vma=False,
    )
```

```python
import functools
import math

import jax
import jax.numpy as jnp
import numpy as np
from jax import lax
from jax.experimental import pallas as pl
from jax.experimental.pallas import tpu as pltpu
from jax.sharding import PartitionSpec as P

EPS = 1e-06
F32 = jnp.float32
BF16 = jnp.bfloat16
MESH = pl.DeviceIdType.MESH
STEP = 256
PARTS = 2


def split(array):
    high = array.astype(BF16)
    return high, (array - high.astype(array.dtype)).astype(BF16)


def dft_matrices(block):
    length = 2 * block
    freq = np.concatenate([np.arange(0, block, 2), np.arange(1, block, 2)])
    at = np.arange(block)
    angle = 2.0 * np.pi * ((freq[:, None] * at[None, :]) % length) / length
    sign = np.where(at % 2 == 0, 1.0, -1.0)
    real, imag = np.cos(angle), -np.sin(angle)
    imag[0] = sign
    forward = np.concatenate([real, imag], 0)
    back = np.concatenate([2.0 * real, 2.0 * imag], 0)
    back[0] *= 0.5
    back[block] *= 0.5
    back = back.T / length

    def parts(matrix):
        matrix = matrix.astype(np.float32)
        high = matrix.astype(jnp.bfloat16)
        low = (matrix - high.astype(np.float32)).astype(jnp.bfloat16)
        return high, low

    fh, fl = parts(forward)
    bh, bl = parts(back)
    return np.concatenate([fh, fl], 1), np.concatenate([bh, bl, bh], 1)


def flip(spec):
    quarter = spec.shape[0] // 4
    return jnp.concatenate(
        [spec[:quarter], -spec[quarter : 2 * quarter], spec[2 * quarter : 3 * quarter], -spec[3 * quarter :]], 0
    )


def product(a, b, conj):
    half = a.shape[0] // 2
    ar, ai, br, bi = a[:half], a[half:], b[:half], b[half:]
    first = lax.broadcasted_iota(jnp.int32, ar.shape, 0) == 0
    rr, ii = ar * br, ai * bi
    if conj:
        real = jnp.where(first, rr, rr + ii)
        imag = jnp.where(first, ii, ai * br - ar * bi)
    else:
        real = jnp.where(first, rr, rr - ii)
        imag = jnp.where(first, ii, ai * br + ar * bi)
    return jnp.concatenate([real, imag], 0)


def kernel(n, t, inside, *refs):
    (q_ref, k_ref, v_ref, f_ref, gain_ref, go_ref, forward_ref, back_ref) = refs[:8]
    outs = refs[8:13]
    gg_ref = refs[13]
    (tail, before, head, after, filt, win, gcs, conv, sq, dots, stat, stat_in, fs, rs_in, red, ag_in, gsend, g_in) = refs[14:32]
    mixed_ref, gq_ref, gk_ref, gv_ref, gf_ref = refs[32:37]
    (t_send, t_recv, h_send, h_recv, s_send, s_recv, r_send, r_recv, a_send, a_recv, g_send, g_recv, o_sem) = refs[37:]
    rows, cols = q_ref.shape
    taps = f_ref.shape[0]
    blocks = rows // taps
    steps = cols // STEP
    part_steps = steps // PARTS
    width = cols * t
    scale = 1.0 / math.sqrt(rows * n)
    me, tp = lax.axis_index("ctx"), lax.axis_index("tp")
    has_prev, has_next = me > 0, me < n - 1

    def leave(i):
        return pltpu.make_async_copy((mixed_ref, gq_ref, gk_ref, gv_ref, gf_ref)[i], outs[i], o_sem.at[i])

    barrier = pltpu.get_barrier_semaphore()

    def greet(axis, peer):
        pl.semaphore_signal(barrier, inc=1, device_id={axis: peer}, device_id_type=MESH)

    for d in range(1, t):
        greet("tp", lax.rem(tp + d, t))
    pl.when(has_prev)(lambda: greet("ctx", me - 1))
    pl.when(has_next)(lambda: greet("ctx", me + 1))
    if inside:
        for d in range(1, n):
            peer = lax.rem(me + d, n)
            far = jnp.logical_and(peer != me + 1, peer != me - 1)
            pl.when(far)(lambda peer=peer: greet("ctx", peer))
        pl.semaphore_wait(barrier, t - 1 + n - 1)
    else:
        pl.semaphore_wait(barrier, t - 1)
        pl.when(has_prev)(lambda: pl.semaphore_wait(barrier, 1))
        pl.when(has_next)(lambda: pl.semaphore_wait(barrier, 1))

    def remote(src, dst, send, recv, axis, peer):
        return pltpu.make_async_remote_copy(
            src_ref=src, dst_ref=dst, send_sem=send, recv_sem=recv,
            device_id={axis: peer}, device_id_type=MESH,
        )

    def tail_copy(c):
        return remote(tail.at[c], before.at[c], t_send.at[c], t_recv.at[c], "ctx", me + 1)

    def head_copy(c):
        return remote(head.at[c], after.at[c], h_send.at[c], h_recv.at[c], "ctx", me - 1)

    def to_spec(block):
        return jnp.dot(forward_ref[...], jnp.concatenate([block, block], 0), preferred_element_type=F32)

    def from_spec(spec):
        high, low = split(spec)
        return jnp.dot(back_ref[...], jnp.concatenate([high, high, low], 0), preferred_element_type=F32)

    def part(b):
        return pl.ds(b * taps, taps)

    def at(c):
        return pl.ds(pl.multiple_of(c * STEP, STEP), STEP)

    def key_value(b, c):
        return (k_ref[part(b), at(c)].astype(F32) * v_ref[part(b), at(c)].astype(F32)).astype(BF16)

    @pl.loop(0, steps)
    def _(c):
        tail[c] = key_value(blocks - 1, c)
        pl.when(has_next)(lambda: tail_copy(c).start())

    sq[...] = jnp.zeros_like(sq)
    dots[...] = jnp.zeros_like(dots)

    def forward_block(b, c):
        out = from_spec(product(win[c, b], filt[c], False))
        conv[c, part(b)] = out
        gated = q_ref[part(b), at(c)].astype(F32) * out
        graded = go_ref[part(b), at(c)].astype(F32) * gain_ref[:, at(c)] * gated
        square = gated * gated
        for i in range(STEP // 128):
            sq[part(b)] += square[:, i * 128 : (i + 1) * 128]
            dots[part(b)] += graded[:, i * 128 : (i + 1) * 128]

    @pl.loop(0, steps)
    def _(c):
        filt[c] = to_spec(f_ref[:, at(c)])
        spec = to_spec(key_value(0, c))
        win[c, 0] = spec
        for b in range(1, blocks):
            last, spec = spec, to_spec(key_value(b, c))
            win[c, b] = spec + flip(last)
            forward_block(b, c)

    @pl.when(jnp.logical_not(has_prev))
    def _():
        before[...] = jnp.zeros_like(before)

    @pl.loop(0, steps)
    def _(c):
        pl.when(has_prev)(lambda: tail_copy(c).wait_recv())
        win[c, 0] += flip(to_spec(before[c]))
        forward_block(0, c)

    lane = lax.broadcasted_iota(jnp.int32, (rows, 128), 1)
    sums = jnp.where(lane == 0, jnp.sum(sq[...], 1, keepdims=True), jnp.sum(dots[...], 1, keepdims=True))
    stat[...] = sums.T[:8]

    def stat_copy(d):
        return remote(stat, stat_in.at[d - 1], s_send.at[d - 1], s_recv.at[d - 1], "tp", lax.rem(tp + d, t))

    for d in range(1, t):
        stat_copy(d).start()
    total = stat[...]
    for d in range(1, t):
        stat_copy(d).wait_recv()
        total += stat_in[d - 1]
    total = jnp.concatenate([total] * 16, 0).T
    inv_rms = lax.rsqrt(total[:, 0:1] / width + EPS)
    row_mean = total[:, 1:2] * inv_rms / width
    sq[...] = jnp.broadcast_to(inv_rms, sq.shape)
    dots[...] = jnp.broadcast_to(row_mean, dots.shape)

    def backward_block(b, c):
        inv, mean = sq[part(b), 0:1], dots[part(b), 0:1]
        query = q_ref[part(b), at(c)].astype(F32)
        grad = go_ref[part(b), at(c)].astype(F32)
        gain = gain_ref[:, at(c)]
        out = conv[c, part(b)]
        normed = query * out * inv
        mixed_ref[part(b), at(c)] = (normed * gain).astype(BF16)
        gated = (grad * gain - normed * mean) * inv
        gq_ref[part(b), at(c)] = (gated * out).astype(BF16)
        return (gated * query).astype(BF16), jnp.sum(grad * normed, 0, keepdims=True)

    def backward_step(c):
        grad_conv, gain_sum = backward_block(0, c)
        head[c] = grad_conv
        pl.when(has_prev)(lambda: head_copy(c).start())
        spec = to_spec(grad_conv)
        gcs[c, 0] = spec
        gf = product(spec, win[c, 0], True)
        for b in range(1, blocks):
            grad_conv, more = backward_block(b, c)
            gain_sum += more
            spec = to_spec(grad_conv)
            gcs[c, b] = spec
            gcs[c, b - 1] += flip(spec)
            gf += product(spec, win[c, b], True)
        gf = from_spec(gf) * scale
        gsend[:, at(c)] = gain_sum * scale
        if inside:
            size = taps // n
            rounded = gf.astype(BF16)
            for r in range(n):
                fs[c // part_steps, r, :, at(c % part_steps)] = rounded[r * size : (r + 1) * size]
        else:
            gf_ref[:, at(c)] = gf

    def rs_copy(h, d):
        peer = lax.rem(me + d, n)
        return remote(fs.at[h, peer], rs_in.at[h, d - 1], r_send.at[h, d - 1], r_recv.at[h, d - 1], "ctx", peer)

    def ag_copy(h, d):
        peer = lax.rem(me + d, n)
        return remote(red.at[h], ag_in.at[h, d - 1], a_send.at[h, d - 1], a_recv.at[h, d - 1], "ctx", peer)

    def gain_copy(d):
        peer = lax.rem(me + d, n)
        return remote(gsend, g_in.at[d - 1], g_send.at[d - 1], g_recv.at[d - 1], "ctx", peer)

    for h in range(PARTS):
        pl.loop(h * part_steps, (h + 1) * part_steps)(backward_step)
        if inside:
            for d in range(1, n):
                rs_copy(h, d).start()
    leave(0).start()
    leave(1).start()
    if inside:
        for d in range(1, n):
            gain_copy(d).start()

    def last_block(b, c):
        grad_kv = from_spec(product(gcs[c, b], filt[c], True))
        gk_ref[part(b), at(c)] = (grad_kv * v_ref[part(b), at(c)].astype(F32)).astype(BF16)
        gv_ref[part(b), at(c)] = (grad_kv * k_ref[part(b), at(c)].astype(F32)).astype(BF16)

    @pl.loop(0, steps)
    def _(c):
        for b in range(blocks - 1):
            last_block(b, c)

    if inside:
        size = taps // n
        for h in range(PARTS):
            for d in range(1, n):
                rs_copy(h, d).wait_recv()
            whole = fs[h, me].astype(F32)
            for d in range(1, n):
                whole += rs_in[h, d - 1].astype(F32)
            red[h] = whole.astype(BF16)
            for d in range(1, n):
                ag_copy(h, d).start()

    @pl.when(jnp.logical_not(has_next))
    def _():
        after[...] = jnp.zeros_like(after)

    @pl.loop(0, steps)
    def _(c):
        pl.when(has_next)(lambda: head_copy(c).wait_recv())
        gcs[c, blocks - 1] += flip(to_spec(after[c]))
        last_block(blocks - 1, c)

    leave(2).start()
    leave(3).start()
    if inside:
        gain_sum = gsend[...]
        for d in range(1, n):
            gain_copy(d).wait_recv()
            gain_sum += g_in[d - 1]
        gg_ref[...] = gain_sum
        for h in range(PARTS):
            span = pl.ds(h * part_steps * STEP, part_steps * STEP)
            gf_ref[pl.ds(pl.multiple_of(me * size, size), size), span] = red[h].astype(F32)
            for d in range(1, n):
                owner = lax.rem(me + n - d, n)
                ag_copy(h, d).wait_recv()
                gf_ref[pl.ds(pl.multiple_of(owner * size, size), size), span] = ag_in[h, d - 1].astype(F32)
        leave(4).start()
        for d in range(1, n):
            gain_copy(d).wait_send()
            for h in range(PARTS):
                rs_copy(h, d).wait_send()
                ag_copy(h, d).wait_send()
    else:
        leave(4).start()
        gg_ref[...] = gsend[...]
    for d in range(1, t):
        stat_copy(d).wait_send()

    @pl.loop(0, steps)
    def _(c):
        pl.when(has_next)(lambda: tail_copy(c).wait_send())
        pl.when(has_prev)(lambda: head_copy(c).wait_send())

    for i in range(5):
        leave(i).wait()


def copies(*refs):
    moves = [pltpu.make_async_copy(refs[i], refs[5 + i], refs[10].at[i]) for i in range(5)]
    for move in moves:
        move.start()
    for move in moves:
        move.wait()


def on_device(query_proj, key_proj, value_proj, filters, norm_gain, grad_out):
    rows, cols = query_proj.shape
    taps = filters.shape[0]
    n, t = lax.axis_size("ctx"), lax.axis_size("tp")
    inside = taps % (16 * n) == 0
    size, peers = (taps // n, n - 1) if inside else (16, 1)
    blocks, steps = rows // taps, cols // STEP
    forward, back = dft_matrices(taps)
    wide = jax.ShapeDtypeStruct((rows, cols), BF16)
    mem = pl.BlockSpec(memory_space=pltpu.VMEM)
    dma = pltpu.SemaphoreType.DMA
    outs = pl.pallas_call(
        functools.partial(kernel, n, t, inside),
        out_shape=(wide, wide, wide, wide,
                   jax.ShapeDtypeStruct((taps, cols), F32), jax.ShapeDtypeStruct((1, cols), F32)),
        in_specs=[mem] * 8,
        out_specs=(pl.BlockSpec(memory_space=pl.ANY),) * 5 + (mem,),
        scratch_shapes=[
            pltpu.VMEM((steps, taps, STEP), BF16),
            pltpu.VMEM((steps, taps, STEP), BF16),
            pltpu.VMEM((steps, taps, STEP), BF16),
            pltpu.VMEM((steps, taps, STEP), BF16),
            pltpu.VMEM((steps, 2 * taps, STEP), F32),
            pltpu.VMEM((steps, blocks, 2 * taps, STEP), F32),
            pltpu.VMEM((steps, blocks, 2 * taps, STEP), F32),
            pltpu.VMEM((steps, rows, STEP), F32),
            pltpu.VMEM((rows, 128), F32),
            pltpu.VMEM((rows, 128), F32),
            pltpu.VMEM((8, rows), F32),
            pltpu.VMEM((t - 1, 8, rows), F32),
            pltpu.VMEM((PARTS, n if inside else 1, size, cols // PARTS), BF16),
            pltpu.VMEM((PARTS, peers, size, cols // PARTS), BF16),
            pltpu.VMEM((PARTS, size, cols // PARTS), BF16),
            pltpu.VMEM((PARTS, peers, size, cols // PARTS), BF16),
            pltpu.VMEM((1, cols), F32),
            pltpu.VMEM((peers, 1, cols), F32),
        ]
        + [pltpu.VMEM((rows, cols), BF16)] * 4 + [pltpu.VMEM((taps, cols), F32)]
        + [dma((steps,))] * 4 + [dma((t - 1,))] * 2 + [dma((PARTS, peers))] * 4 + [dma((peers,))] * 2
        + [dma((5,))],
        compiler_params=pltpu.CompilerParams(
            collective_id=0, has_side_effects=True, vmem_limit_bytes=56 * 1024 * 1024
        ),
        cost_estimate=pl.CostEstimate(flops=4_000_000_000, bytes_accessed=10_000_000, transcendentals=0),
    )(query_proj, key_proj, value_proj, filters, norm_gain[None], grad_out,
      jnp.asarray(forward), jnp.asarray(back))
    hbm = pl.BlockSpec(memory_space=pl.ANY)
    mixed, grad_query, grad_key, grad_value, grad_filter = pl.pallas_call(
        copies,
        out_shape=tuple(jax.ShapeDtypeStruct(a.shape, a.dtype) for a in outs[:5]),
        in_specs=[hbm] * 5,
        out_specs=(hbm,) * 5,
        scratch_shapes=[dma((5,))],
    )(*outs[:5])
    grad_gain = outs[5]
    if not inside:
        grad_filter, grad_gain = lax.psum((grad_filter, grad_gain), "ctx")
    return (mixed, grad_query, grad_key, grad_value, grad_filter, grad_gain[0])


def solution(mesh):
    placed = (
        P("ctx", "tp"),
        P("ctx", "tp"),
        P("ctx", "tp"),
        P(None, "tp"),
        P("tp"),
        P("ctx", "tp"),
    )
    return jax.shard_map(
        on_device,
        mesh=mesh,
        in_specs=placed,
        out_specs=(
            P("ctx", "tp"),
            P("ctx", "tp"),
            P("ctx", "tp"),
            P("ctx", "tp"),
            P(None, "tp"),
            P("tp"),
        ),
        check_vma=False,
    )
```

```python
import functools
import math

import jax
import jax.numpy as jnp
import numpy as np
from jax import lax
from jax.experimental import pallas as pl
from jax.experimental.pallas import tpu as pltpu
from jax.sharding import PartitionSpec as P

EPS = 1e-06
F32 = jnp.float32
BF16 = jnp.bfloat16
MESH = pl.DeviceIdType.MESH
STEP = 256
PARTS = 2


def split(array):
    high = array.astype(BF16)
    return high, (array - high.astype(array.dtype)).astype(BF16)


def dft_matrices(block):
    length = 2 * block
    freq = np.concatenate([np.arange(0, block, 2), np.arange(1, block, 2)])
    at = np.arange(block)
    angle = 2.0 * np.pi * ((freq[:, None] * at[None, :]) % length) / length
    sign = np.where(at % 2 == 0, 1.0, -1.0)
    real, imag = np.cos(angle), -np.sin(angle)
    imag[0] = sign
    forward = np.concatenate([real, imag], 0)
    back = np.concatenate([2.0 * real, 2.0 * imag], 0)
    back[0] *= 0.5
    back[block] *= 0.5
    back = back.T / length

    def parts(matrix):
        matrix = matrix.astype(np.float32)
        high = matrix.astype(jnp.bfloat16)
        low = (matrix - high.astype(np.float32)).astype(jnp.bfloat16)
        return high, low

    fh, fl = parts(forward)
    bh, bl = parts(back)
    return np.concatenate([fh, fl], 1), np.concatenate([bh, bl, bh], 1)


def flip(spec):
    quarter = spec.shape[0] // 4
    return jnp.concatenate(
        [spec[:quarter], -spec[quarter : 2 * quarter], spec[2 * quarter : 3 * quarter], -spec[3 * quarter :]], 0
    )


def product(a, b, conj):
    half = a.shape[0] // 2
    ar, ai, br, bi = a[:half], a[half:], b[:half], b[half:]
    first = lax.broadcasted_iota(jnp.int32, ar.shape, 0) == 0
    rr, ii = ar * br, ai * bi
    if conj:
        real = jnp.where(first, rr, rr + ii)
        imag = jnp.where(first, ii, ai * br - ar * bi)
    else:
        real = jnp.where(first, rr, rr - ii)
        imag = jnp.where(first, ii, ai * br + ar * bi)
    return jnp.concatenate([real, imag], 0)


def kernel(n, t, inside, *refs):
    (q_ref, k_ref, v_ref, f_ref, gain_ref, go_ref, forward_ref, back_ref) = refs[:8]
    outs = refs[8:13]
    gg_ref = refs[13]
    (tail, before, head, after, filt, win, gcs, conv, sq, dots, stat, stat_in, fs, rs_in, red, ag_in, gsend, g_in) = refs[14:32]
    mixed_ref, gq_ref, gk_ref, gv_ref, gf_ref = refs[32:37]
    (t_send, t_recv, h_send, h_recv, s_send, s_recv, r_send, r_recv, a_send, a_recv, g_send, g_recv, o_sem) = refs[37:]
    rows, cols = q_ref.shape
    taps = f_ref.shape[0]
    blocks = rows // taps
    steps = cols // STEP
    part_steps = steps // PARTS
    width = cols * t
    scale = 1.0 / math.sqrt(rows * n)
    me, tp = lax.axis_index("ctx"), lax.axis_index("tp")
    has_prev, has_next = me > 0, me < n - 1

    def leave(i):
        return pltpu.make_async_copy((mixed_ref, gq_ref, gk_ref, gv_ref, gf_ref)[i], outs[i], o_sem.at[i])

    barrier = pltpu.get_barrier_semaphore()

    def greet(axis, peer):
        pl.semaphore_signal(barrier, inc=1, device_id={axis: peer}, device_id_type=MESH)

    for d in range(1, t):
        greet("tp", lax.rem(tp + d, t))
    pl.when(has_prev)(lambda: greet("ctx", me - 1))
    pl.when(has_next)(lambda: greet("ctx", me + 1))
    if inside:
        for d in range(1, n):
            peer = lax.rem(me + d, n)
            far = jnp.logical_and(peer != me + 1, peer != me - 1)
            pl.when(far)(lambda peer=peer: greet("ctx", peer))
        pl.semaphore_wait(barrier, t - 1 + n - 1)
    else:
        pl.semaphore_wait(barrier, t - 1)
        pl.when(has_prev)(lambda: pl.semaphore_wait(barrier, 1))
        pl.when(has_next)(lambda: pl.semaphore_wait(barrier, 1))

    def remote(src, dst, send, recv, axis, peer):
        return pltpu.make_async_remote_copy(
            src_ref=src, dst_ref=dst, send_sem=send, recv_sem=recv,
            device_id={axis: peer}, device_id_type=MESH,
        )

    def tail_copy(c):
        return remote(tail.at[c], before.at[c], t_send.at[c], t_recv.at[c], "ctx", me + 1)

    def head_copy(c):
        return remote(head.at[c], after.at[c], h_send.at[c], h_recv.at[c], "ctx", me - 1)

    def to_spec(block):
        return jnp.dot(forward_ref[...], jnp.concatenate([block, block], 0), preferred_element_type=F32)

    def from_spec(spec):
        high, low = split(spec)
        return jnp.dot(back_ref[...], jnp.concatenate([high, high, low], 0), preferred_element_type=F32)

    def part(b):
        return pl.ds(b * taps, taps)

    def at(c):
        return pl.ds(pl.multiple_of(c * STEP, STEP), STEP)

    def key_value(b, c):
        return (k_ref[part(b), at(c)].astype(F32) * v_ref[part(b), at(c)].astype(F32)).astype(BF16)

    @pl.loop(0, steps)
    def _(c):
        tail[c] = key_value(blocks - 1, c)
        pl.when(has_next)(lambda: tail_copy(c).start())

    sq[...] = jnp.zeros_like(sq)
    dots[...] = jnp.zeros_like(dots)

    def forward_block(b, c):
        out = from_spec(product(win[c, b], filt[c], False))
        conv[c, part(b)] = out
        gated = q_ref[part(b), at(c)].astype(F32) * out
        graded = go_ref[part(b), at(c)].astype(F32) * gain_ref[:, at(c)] * gated
        square = gated * gated
        for i in range(STEP // 128):
            sq[part(b)] += square[:, i * 128 : (i + 1) * 128]
            dots[part(b)] += graded[:, i * 128 : (i + 1) * 128]

    @pl.loop(0, steps)
    def _(c):
        filt[c] = to_spec(f_ref[:, at(c)])
        spec = to_spec(key_value(0, c))
        win[c, 0] = spec
        for b in range(1, blocks):
            last, spec = spec, to_spec(key_value(b, c))
            win[c, b] = spec + flip(last)
            forward_block(b, c)

    @pl.when(jnp.logical_not(has_prev))
    def _():
        before[...] = jnp.zeros_like(before)

    @pl.loop(0, steps)
    def _(c):
        pl.when(has_prev)(lambda: tail_copy(c).wait_recv())
        win[c, 0] += flip(to_spec(before[c]))
        forward_block(0, c)

    lane = lax.broadcasted_iota(jnp.int32, (rows, 128), 1)
    sums = jnp.where(lane == 0, jnp.sum(sq[...], 1, keepdims=True), jnp.sum(dots[...], 1, keepdims=True))
    stat[...] = sums.T[:8]

    def stat_copy(d):
        return remote(stat, stat_in.at[d - 1], s_send.at[d - 1], s_recv.at[d - 1], "tp", lax.rem(tp + d, t))

    for d in range(1, t):
        stat_copy(d).start()
    total = stat[...]
    for d in range(1, t):
        stat_copy(d).wait_recv()
        total += stat_in[d - 1]
    total = jnp.concatenate([total] * 16, 0).T
    inv_rms = lax.rsqrt(total[:, 0:1] / width + EPS)
    row_mean = total[:, 1:2] * inv_rms / width
    sq[...] = jnp.broadcast_to(inv_rms, sq.shape)
    dots[...] = jnp.broadcast_to(row_mean, dots.shape)

    def backward_block(b, c):
        inv, mean = sq[part(b), 0:1], dots[part(b), 0:1]
        query = q_ref[part(b), at(c)].astype(F32)
        grad = go_ref[part(b), at(c)].astype(F32)
        gain = gain_ref[:, at(c)]
        out = conv[c, part(b)]
        normed = query * out * inv
        mixed_ref[part(b), at(c)] = (normed * gain).astype(BF16)
        gated = (grad * gain - normed * mean) * inv
        gq_ref[part(b), at(c)] = (gated * out).astype(BF16)
        return (gated * query).astype(BF16), jnp.sum(grad * normed, 0, keepdims=True)

    def backward_step(c):
        grad_conv, gain_sum = backward_block(0, c)
        head[c] = grad_conv
        pl.when(has_prev)(lambda: head_copy(c).start())
        spec = to_spec(grad_conv)
        gcs[c, 0] = spec
        gf = product(spec, win[c, 0], True)
        for b in range(1, blocks):
            grad_conv, more = backward_block(b, c)
            gain_sum += more
            spec = to_spec(grad_conv)
            gcs[c, b] = spec
            gcs[c, b - 1] += flip(spec)
            gf += product(spec, win[c, b], True)
        gf = from_spec(gf) * scale
        gsend[:, at(c)] = gain_sum * scale
        if inside:
            size = taps // n
            rounded = gf.astype(BF16)
            for r in range(n):
                fs[c // part_steps, r, :, at(c % part_steps)] = rounded[r * size : (r + 1) * size]
        else:
            gf_ref[:, at(c)] = gf

    def rs_copy(h, d):
        peer = lax.rem(me + d, n)
        return remote(fs.at[h, peer], rs_in.at[h, d - 1], r_send.at[h, d - 1], r_recv.at[h, d - 1], "ctx", peer)

    def ag_copy(h, d):
        peer = lax.rem(me + d, n)
        return remote(red.at[h], ag_in.at[h, d - 1], a_send.at[h, d - 1], a_recv.at[h, d - 1], "ctx", peer)

    def gain_copy(d):
        peer = lax.rem(me + d, n)
        return remote(gsend, g_in.at[d - 1], g_send.at[d - 1], g_recv.at[d - 1], "ctx", peer)

    for h in range(PARTS):
        pl.loop(h * part_steps, (h + 1) * part_steps)(backward_step)
        if inside:
            for d in range(1, n):
                rs_copy(h, d).start()
    leave(0).start()
    leave(1).start()
    if inside:
        for d in range(1, n):
            gain_copy(d).start()

    def last_block(b, c):
        grad_kv = from_spec(product(gcs[c, b], filt[c], True))
        gk_ref[part(b), at(c)] = (grad_kv * v_ref[part(b), at(c)].astype(F32)).astype(BF16)
        gv_ref[part(b), at(c)] = (grad_kv * k_ref[part(b), at(c)].astype(F32)).astype(BF16)

    @pl.loop(0, steps)
    def _(c):
        for b in range(blocks - 1):
            last_block(b, c)

    if inside:
        size = taps // n
        for h in range(PARTS):
            for d in range(1, n):
                rs_copy(h, d).wait_recv()
            whole = fs[h, me].astype(F32)
            for d in range(1, n):
                whole += rs_in[h, d - 1].astype(F32)
            red[h] = whole.astype(BF16)
            for d in range(1, n):
                ag_copy(h, d).start()

    @pl.when(jnp.logical_not(has_next))
    def _():
        after[...] = jnp.zeros_like(after)

    @pl.loop(0, steps)
    def _(c):
        pl.when(has_next)(lambda: head_copy(c).wait_recv())
        gcs[c, blocks - 1] += flip(to_spec(after[c]))
        last_block(blocks - 1, c)

    leave(2).start()
    leave(3).start()
    if inside:
        gain_sum = gsend[...]
        for d in range(1, n):
            gain_copy(d).wait_recv()
            gain_sum += g_in[d - 1]
        gg_ref[...] = gain_sum
        for h in range(PARTS):
            span = pl.ds(h * part_steps * STEP, part_steps * STEP)
            gf_ref[pl.ds(pl.multiple_of(me * size, size), size), span] = red[h].astype(F32)
            for d in range(1, n):
                owner = lax.rem(me + n - d, n)
                ag_copy(h, d).wait_recv()
                gf_ref[pl.ds(pl.multiple_of(owner * size, size), size), span] = ag_in[h, d - 1].astype(F32)
        leave(4).start()
        for d in range(1, n):
            gain_copy(d).wait_send()
            for h in range(PARTS):
                rs_copy(h, d).wait_send()
                ag_copy(h, d).wait_send()
    else:
        leave(4).start()
        gg_ref[...] = gsend[...]
    for d in range(1, t):
        stat_copy(d).wait_send()

    @pl.loop(0, steps)
    def _(c):
        pl.when(has_next)(lambda: tail_copy(c).wait_send())
        pl.when(has_prev)(lambda: head_copy(c).wait_send())

    for i in range(5):
        leave(i).wait()


def copies(*refs):
    sources, source_gain, targets, target_gain = refs[:5], refs[5], refs[6:11], refs[11]
    held, in_sem, out_sem = refs[12:17], refs[17], refs[18]
    inward, outward = [], []
    for i in range(5):
        half = sources[i].shape[0] // 2
        for h in range(2):
            span = pl.ds(h * half, half)
            sems = in_sem.at[2 * i + h], out_sem.at[2 * i + h]
            inward.append(pltpu.make_async_copy(sources[i].at[span], held[i].at[span], sems[0]))
            outward.append(pltpu.make_async_copy(held[i].at[span], targets[i].at[span], sems[1]))
    for move in inward:
        move.start()
    target_gain[...] = source_gain[...]
    for first, second in zip(inward, outward):
        first.wait()
        second.start()
    for move in outward:
        move.wait()


def on_device(query_proj, key_proj, value_proj, filters, norm_gain, grad_out):
    rows, cols = query_proj.shape
    taps = filters.shape[0]
    n, t = lax.axis_size("ctx"), lax.axis_size("tp")
    inside = taps % (16 * n) == 0
    size, peers = (taps // n, n - 1) if inside else (16, 1)
    blocks, steps = rows // taps, cols // STEP
    forward, back = dft_matrices(taps)
    wide = jax.ShapeDtypeStruct((rows, cols), BF16)
    mem = pl.BlockSpec(memory_space=pltpu.VMEM)
    dma = pltpu.SemaphoreType.DMA
    outs = pl.pallas_call(
        functools.partial(kernel, n, t, inside),
        out_shape=(wide, wide, wide, wide,
                   jax.ShapeDtypeStruct((taps, cols), F32), jax.ShapeDtypeStruct((1, cols), F32)),
        in_specs=[mem] * 8,
        out_specs=(pl.BlockSpec(memory_space=pl.ANY),) * 5 + (mem,),
        scratch_shapes=[
            pltpu.VMEM((steps, taps, STEP), BF16),
            pltpu.VMEM((steps, taps, STEP), BF16),
            pltpu.VMEM((steps, taps, STEP), BF16),
            pltpu.VMEM((steps, taps, STEP), BF16),
            pltpu.VMEM((steps, 2 * taps, STEP), F32),
            pltpu.VMEM((steps, blocks, 2 * taps, STEP), F32),
            pltpu.VMEM((steps, blocks, 2 * taps, STEP), F32),
            pltpu.VMEM((steps, rows, STEP), F32),
            pltpu.VMEM((rows, 128), F32),
            pltpu.VMEM((rows, 128), F32),
            pltpu.VMEM((8, rows), F32),
            pltpu.VMEM((t - 1, 8, rows), F32),
            pltpu.VMEM((PARTS, n if inside else 1, size, cols // PARTS), BF16),
            pltpu.VMEM((PARTS, peers, size, cols // PARTS), BF16),
            pltpu.VMEM((PARTS, size, cols // PARTS), BF16),
            pltpu.VMEM((PARTS, peers, size, cols // PARTS), BF16),
            pltpu.VMEM((1, cols), F32),
            pltpu.VMEM((peers, 1, cols), F32),
        ]
        + [pltpu.VMEM((rows, cols), BF16)] * 4 + [pltpu.VMEM((taps, cols), F32)]
        + [dma((steps,))] * 4 + [dma((t - 1,))] * 2 + [dma((PARTS, peers))] * 4 + [dma((peers,))] * 2
        + [dma((5,))],
        compiler_params=pltpu.CompilerParams(
            collective_id=0, has_side_effects=True, vmem_limit_bytes=56 * 1024 * 1024
        ),
        cost_estimate=pl.CostEstimate(flops=4_000_000_000, bytes_accessed=10_000_000, transcendentals=0),
    )(query_proj, key_proj, value_proj, filters, norm_gain[None], grad_out,
      jnp.asarray(forward), jnp.asarray(back))
    hbm = pl.BlockSpec(memory_space=pl.ANY)
    mixed, grad_query, grad_key, grad_value, grad_filter, grad_gain = pl.pallas_call(
        copies,
        out_shape=tuple(jax.ShapeDtypeStruct(a.shape, a.dtype) for a in outs),
        in_specs=[hbm] * 5 + [mem],
        out_specs=(hbm,) * 5 + (mem,),
        scratch_shapes=[pltpu.VMEM(a.shape, a.dtype) for a in outs[:5]] + [dma((10,))] * 2,
        compiler_params=pltpu.CompilerParams(vmem_limit_bytes=24 * 1024 * 1024),
    )(*outs)
    if not inside:
        grad_filter, grad_gain = lax.psum((grad_filter, grad_gain), "ctx")
    return (mixed, grad_query, grad_key, grad_value, grad_filter, grad_gain[0])


def solution(mesh):
    placed = (
        P("ctx", "tp"),
        P("ctx", "tp"),
        P("ctx", "tp"),
        P(None, "tp"),
        P("tp"),
        P("ctx", "tp"),
    )
    return jax.shard_map(
        on_device,
        mesh=mesh,
        in_specs=placed,
        out_specs=(
            P("ctx", "tp"),
            P("ctx", "tp"),
            P("ctx", "tp"),
            P("ctx", "tp"),
            P(None, "tp"),
            P("tp"),
        ),
        check_vma=False,
    )
```

```python
import functools
import math

import jax
import jax.numpy as jnp
import numpy as np
from jax import lax
from jax.experimental import pallas as pl
from jax.experimental.pallas import tpu as pltpu
from jax.sharding import PartitionSpec as P

EPS = 1e-06
F32 = jnp.float32
BF16 = jnp.bfloat16
MESH = pl.DeviceIdType.MESH
STEP = 256
PARTS = 2


def split(array):
    high = array.astype(BF16)
    return high, (array - high.astype(array.dtype)).astype(BF16)


def dft_matrices(block):
    length = 2 * block
    freq = np.concatenate([np.arange(0, block, 2), np.arange(1, block, 2)])
    at = np.arange(block)
    angle = 2.0 * np.pi * ((freq[:, None] * at[None, :]) % length) / length
    sign = np.where(at % 2 == 0, 1.0, -1.0)
    real, imag = np.cos(angle), -np.sin(angle)
    imag[0] = sign
    forward = np.concatenate([real, imag], 0)
    back = np.concatenate([2.0 * real, 2.0 * imag], 0)
    back[0] *= 0.5
    back[block] *= 0.5
    back = back.T / length

    def parts(matrix):
        matrix = matrix.astype(np.float32)
        high = matrix.astype(jnp.bfloat16)
        low = (matrix - high.astype(np.float32)).astype(jnp.bfloat16)
        return high, low

    fh, fl = parts(forward)
    bh, bl = parts(back)
    return np.concatenate([fh, fl], 1), np.concatenate([bh, bl, bh], 1)


def flip(spec):
    quarter = spec.shape[0] // 4
    return jnp.concatenate(
        [spec[:quarter], -spec[quarter : 2 * quarter], spec[2 * quarter : 3 * quarter], -spec[3 * quarter :]], 0
    )


def product(a, b, conj):
    half = a.shape[0] // 2
    ar, ai, br, bi = a[:half], a[half:], b[:half], b[half:]
    first = lax.broadcasted_iota(jnp.int32, ar.shape, 0) == 0
    rr, ii = ar * br, ai * bi
    if conj:
        real = jnp.where(first, rr, rr + ii)
        imag = jnp.where(first, ii, ai * br - ar * bi)
    else:
        real = jnp.where(first, rr, rr - ii)
        imag = jnp.where(first, ii, ai * br + ar * bi)
    return jnp.concatenate([real, imag], 0)


def kernel(n, t, inside, *refs):
    (q_ref, k_ref, v_ref, f_ref, gain_ref, go_ref, forward_ref, back_ref) = refs[:8]
    outs = refs[8:13]
    gg_ref = refs[13]
    (tail, before, head, after, filt, win, gcs, conv, sq, dots, stat, stat_in, fs, rs_in, red, ag_in, gsend, g_in) = refs[14:32]
    mixed_ref, gq_ref, gk_ref, gv_ref, gf_ref = refs[32:37]
    (t_send, t_recv, h_send, h_recv, s_send, s_recv, r_send, r_recv, a_send, a_recv, g_send, g_recv, o_sem) = refs[37:]
    rows, cols = q_ref.shape
    taps = f_ref.shape[0]
    blocks = rows // taps
    steps = cols // STEP
    part_steps = steps // PARTS
    width = cols * t
    scale = 1.0 / math.sqrt(rows * n)
    me, tp = lax.axis_index("ctx"), lax.axis_index("tp")
    has_prev, has_next = me > 0, me < n - 1

    def leave(i):
        return pltpu.make_async_copy((mixed_ref, gq_ref, gk_ref, gv_ref, gf_ref)[i], outs[i], o_sem.at[i])

    barrier = pltpu.get_barrier_semaphore()

    def greet(axis, peer):
        pl.semaphore_signal(barrier, inc=1, device_id={axis: peer}, device_id_type=MESH)

    for d in range(1, t):
        greet("tp", lax.rem(tp + d, t))
    pl.when(has_prev)(lambda: greet("ctx", me - 1))
    pl.when(has_next)(lambda: greet("ctx", me + 1))
    if inside:
        for d in range(1, n):
            peer = lax.rem(me + d, n)
            far = jnp.logical_and(peer != me + 1, peer != me - 1)
            pl.when(far)(lambda peer=peer: greet("ctx", peer))
        pl.semaphore_wait(barrier, t - 1 + n - 1)
    else:
        pl.semaphore_wait(barrier, t - 1)
        pl.when(has_prev)(lambda: pl.semaphore_wait(barrier, 1))
        pl.when(has_next)(lambda: pl.semaphore_wait(barrier, 1))

    def remote(src, dst, send, recv, axis, peer):
        return pltpu.make_async_remote_copy(
            src_ref=src, dst_ref=dst, send_sem=send, recv_sem=recv,
            device_id={axis: peer}, device_id_type=MESH,
        )

    def tail_copy(c):
        return remote(tail.at[c], before.at[c], t_send.at[c], t_recv.at[c], "ctx", me + 1)

    def head_copy(c):
        return remote(head.at[c], after.at[c], h_send.at[c], h_recv.at[c], "ctx", me - 1)

    def to_spec(block):
        return jnp.dot(forward_ref[...], jnp.concatenate([block, block], 0), preferred_element_type=F32)

    def from_spec(spec):
        high, low = split(spec)
        return jnp.dot(back_ref[...], jnp.concatenate([high, high, low], 0), preferred_element_type=F32)

    def part(b):
        return pl.ds(b * taps, taps)

    def at(c):
        return pl.ds(pl.multiple_of(c * STEP, STEP), STEP)

    def key_value(b, c):
        return (k_ref[part(b), at(c)].astype(F32) * v_ref[part(b), at(c)].astype(F32)).astype(BF16)

    @pl.loop(0, steps)
    def _(c):
        tail[c] = key_value(blocks - 1, c)
        pl.when(has_next)(lambda: tail_copy(c).start())

    sq[...] = jnp.zeros_like(sq)
    dots[...] = jnp.zeros_like(dots)

    def forward_block(b, c):
        out = from_spec(product(win[c, b], filt[c], False))
        conv[c, part(b)] = out
        gated = q_ref[part(b), at(c)].astype(F32) * out
        graded = go_ref[part(b), at(c)].astype(F32) * gain_ref[:, at(c)] * gated
        square = gated * gated
        for i in range(STEP // 128):
            sq[part(b)] += square[:, i * 128 : (i + 1) * 128]
            dots[part(b)] += graded[:, i * 128 : (i + 1) * 128]

    @pl.loop(0, steps)
    def _(c):
        filt[c] = to_spec(f_ref[:, at(c)])
        spec = to_spec(key_value(0, c))
        win[c, 0] = spec
        for b in range(1, blocks):
            last, spec = spec, to_spec(key_value(b, c))
            win[c, b] = spec + flip(last)
            forward_block(b, c)

    @pl.when(jnp.logical_not(has_prev))
    def _():
        before[...] = jnp.zeros_like(before)

    @pl.loop(0, steps)
    def _(c):
        pl.when(has_prev)(lambda: tail_copy(c).wait_recv())
        win[c, 0] += flip(to_spec(before[c]))
        forward_block(0, c)

    lane = lax.broadcasted_iota(jnp.int32, (rows, 128), 1)
    sums = jnp.where(lane == 0, jnp.sum(sq[...], 1, keepdims=True), jnp.sum(dots[...], 1, keepdims=True))
    stat[...] = sums.T[:8]

    def stat_copy(d):
        return remote(stat, stat_in.at[d - 1], s_send.at[d - 1], s_recv.at[d - 1], "tp", lax.rem(tp + d, t))

    for d in range(1, t):
        stat_copy(d).start()
    total = stat[...]
    for d in range(1, t):
        stat_copy(d).wait_recv()
        total += stat_in[d - 1]
    total = jnp.concatenate([total] * 16, 0).T
    inv_rms = lax.rsqrt(total[:, 0:1] / width + EPS)
    row_mean = total[:, 1:2] * inv_rms / width
    sq[...] = jnp.broadcast_to(inv_rms, sq.shape)
    dots[...] = jnp.broadcast_to(row_mean, dots.shape)

    def backward_block(b, c):
        inv, mean = sq[part(b), 0:1], dots[part(b), 0:1]
        query = q_ref[part(b), at(c)].astype(F32)
        grad = go_ref[part(b), at(c)].astype(F32)
        gain = gain_ref[:, at(c)]
        out = conv[c, part(b)]
        normed = query * out * inv
        mixed_ref[part(b), at(c)] = (normed * gain).astype(BF16)
        gated = (grad * gain - normed * mean) * inv
        gq_ref[part(b), at(c)] = (gated * out).astype(BF16)
        return (gated * query).astype(BF16), jnp.sum(grad * normed, 0, keepdims=True)

    def backward_step(c):
        grad_conv, gain_sum = backward_block(0, c)
        head[c] = grad_conv
        pl.when(has_prev)(lambda: head_copy(c).start())
        spec = to_spec(grad_conv)
        gcs[c, 0] = spec
        gf = product(spec, win[c, 0], True)
        for b in range(1, blocks):
            grad_conv, more = backward_block(b, c)
            gain_sum += more
            spec = to_spec(grad_conv)
            gcs[c, b] = spec
            gcs[c, b - 1] += flip(spec)
            gf += product(spec, win[c, b], True)
        gf = from_spec(gf) * scale
        gsend[:, at(c)] = gain_sum * scale
        if inside:
            size = taps // n
            rounded = gf.astype(BF16)
            for r in range(n):
                fs[c // part_steps, r, :, at(c % part_steps)] = rounded[r * size : (r + 1) * size]
        else:
            gf_ref[:, at(c)] = gf

    def rs_copy(h, d):
        peer = lax.rem(me + d, n)
        return remote(fs.at[h, peer], rs_in.at[h, d - 1], r_send.at[h, d - 1], r_recv.at[h, d - 1], "ctx", peer)

    def ag_copy(h, d):
        peer = lax.rem(me + d, n)
        return remote(red.at[h], ag_in.at[h, d - 1], a_send.at[h, d - 1], a_recv.at[h, d - 1], "ctx", peer)

    def gain_copy(d):
        peer = lax.rem(me + d, n)
        return remote(gsend, g_in.at[d - 1], g_send.at[d - 1], g_recv.at[d - 1], "ctx", peer)

    for h in range(PARTS):
        pl.loop(h * part_steps, (h + 1) * part_steps)(backward_step)
        if inside:
            for d in range(1, n):
                rs_copy(h, d).start()
    leave(0).start()
    leave(1).start()
    if inside:
        for d in range(1, n):
            gain_copy(d).start()

    def last_block(b, c):
        grad_kv = from_spec(product(gcs[c, b], filt[c], True))
        gk_ref[part(b), at(c)] = (grad_kv * v_ref[part(b), at(c)].astype(F32)).astype(BF16)
        gv_ref[part(b), at(c)] = (grad_kv * k_ref[part(b), at(c)].astype(F32)).astype(BF16)

    @pl.loop(0, steps)
    def _(c):
        for b in range(blocks - 1):
            last_block(b, c)

    if inside:
        size = taps // n
        for h in range(PARTS):
            for d in range(1, n):
                rs_copy(h, d).wait_recv()
            whole = fs[h, me].astype(F32)
            for d in range(1, n):
                whole += rs_in[h, d - 1].astype(F32)
            red[h] = whole.astype(BF16)
            for d in range(1, n):
                ag_copy(h, d).start()

    @pl.when(jnp.logical_not(has_next))
    def _():
        after[...] = jnp.zeros_like(after)

    @pl.loop(0, steps)
    def _(c):
        pl.when(has_next)(lambda: head_copy(c).wait_recv())
        gcs[c, blocks - 1] += flip(to_spec(after[c]))
        last_block(blocks - 1, c)

    leave(2).start()
    leave(3).start()
    if inside:
        gain_sum = gsend[...]
        for d in range(1, n):
            gain_copy(d).wait_recv()
            gain_sum += g_in[d - 1]
        gg_ref[...] = gain_sum
        for h in range(PARTS):
            span = pl.ds(h * part_steps * STEP, part_steps * STEP)
            gf_ref[pl.ds(pl.multiple_of(me * size, size), size), span] = red[h].astype(F32)
            for d in range(1, n):
                owner = lax.rem(me + n - d, n)
                ag_copy(h, d).wait_recv()
                gf_ref[pl.ds(pl.multiple_of(owner * size, size), size), span] = ag_in[h, d - 1].astype(F32)
        leave(4).start()
        for d in range(1, n):
            gain_copy(d).wait_send()
            for h in range(PARTS):
                rs_copy(h, d).wait_send()
                ag_copy(h, d).wait_send()
    else:
        leave(4).start()
        gg_ref[...] = gsend[...]
    for d in range(1, t):
        stat_copy(d).wait_send()

    @pl.loop(0, steps)
    def _(c):
        pl.when(has_next)(lambda: tail_copy(c).wait_send())
        pl.when(has_prev)(lambda: head_copy(c).wait_send())

    for i in range(5):
        leave(i).wait()


def copies(*refs):
    sources, source_gain, targets, target_gain = refs[:5], refs[5], refs[6:11], refs[11]
    held, in_sem, out_sem = refs[12:17], refs[17], refs[18]
    inward, outward = [], []
    for i in range(5):
        half = sources[i].shape[0] // 2
        for h in range(2):
            span = pl.ds(h * half, half)
            sems = in_sem.at[2 * i + h], out_sem.at[2 * i + h]
            inward.append(pltpu.make_async_copy(sources[i].at[span], held[i].at[span], sems[0]))
            outward.append(pltpu.make_async_copy(held[i].at[span], targets[i].at[span], sems[1]))
    for move in inward:
        move.start()
    target_gain[...] = source_gain[...]
    for first, second in zip(inward, outward):
        first.wait()
        second.start()
    for move in outward:
        move.wait()


def on_device(query_proj, key_proj, value_proj, filters, norm_gain, grad_out):
    rows, cols = query_proj.shape
    taps = filters.shape[0]
    n, t = lax.axis_size("ctx"), lax.axis_size("tp")
    inside = taps % (16 * n) == 0
    size, peers = (taps // n, n - 1) if inside else (16, 1)
    blocks, steps = rows // taps, cols // STEP
    forward, back = dft_matrices(taps)
    wide = jax.ShapeDtypeStruct((rows, cols), BF16)
    mem = pl.BlockSpec(memory_space=pltpu.VMEM)
    dma = pltpu.SemaphoreType.DMA
    outs = pl.pallas_call(
        functools.partial(kernel, n, t, inside),
        out_shape=(wide, wide, wide, wide,
                   jax.ShapeDtypeStruct((taps, cols), F32), jax.ShapeDtypeStruct((1, cols), F32)),
        in_specs=[mem] * 8,
        out_specs=(pl.BlockSpec(memory_space=pl.ANY),) * 5 + (mem,),
        scratch_shapes=[
            pltpu.VMEM((steps, taps, STEP), BF16),
            pltpu.VMEM((steps, taps, STEP), BF16),
            pltpu.VMEM((steps, taps, STEP), BF16),
            pltpu.VMEM((steps, taps, STEP), BF16),
            pltpu.VMEM((steps, 2 * taps, STEP), F32),
            pltpu.VMEM((steps, blocks, 2 * taps, STEP), F32),
            pltpu.VMEM((steps, blocks, 2 * taps, STEP), F32),
            pltpu.VMEM((steps, rows, STEP), F32),
            pltpu.VMEM((rows, 128), F32),
            pltpu.VMEM((rows, 128), F32),
            pltpu.VMEM((8, rows), F32),
            pltpu.VMEM((t - 1, 8, rows), F32),
            pltpu.VMEM((PARTS, n if inside else 1, size, cols // PARTS), BF16),
            pltpu.VMEM((PARTS, peers, size, cols // PARTS), BF16),
            pltpu.VMEM((PARTS, size, cols // PARTS), BF16),
            pltpu.VMEM((PARTS, peers, size, cols // PARTS), BF16),
            pltpu.VMEM((1, cols), F32),
            pltpu.VMEM((peers, 1, cols), F32),
        ]
        + [pltpu.VMEM((rows, cols), BF16)] * 4 + [pltpu.VMEM((taps, cols), F32)]
        + [dma((steps,))] * 4 + [dma((t - 1,))] * 2 + [dma((PARTS, peers))] * 4 + [dma((peers,))] * 2
        + [dma((5,))],
        compiler_params=pltpu.CompilerParams(
            collective_id=0, has_side_effects=True, vmem_limit_bytes=56 * 1024 * 1024
        ),
        cost_estimate=pl.CostEstimate(flops=4_000_000_000, bytes_accessed=10_000_000, transcendentals=0),
    )(query_proj, key_proj, value_proj, filters, norm_gain[None], grad_out,
      jnp.asarray(forward), jnp.asarray(back))
    hbm = pl.BlockSpec(memory_space=pl.ANY)
    mixed, grad_query, grad_key, grad_value, grad_filter, grad_gain = pl.pallas_call(
        copies,
        out_shape=tuple(jax.ShapeDtypeStruct(a.shape, a.dtype) for a in outs),
        in_specs=[hbm] * 5 + [mem],
        out_specs=(hbm,) * 5 + (mem,),
        scratch_shapes=[pltpu.VMEM(a.shape, a.dtype) for a in outs[:5]] + [dma((10,))] * 2,
        compiler_params=pltpu.CompilerParams(vmem_limit_bytes=56 * 1024 * 1024),
    )(*outs)
    if not inside:
        grad_filter, grad_gain = lax.psum((grad_filter, grad_gain), "ctx")
    return (mixed, grad_query, grad_key, grad_value, grad_filter, grad_gain[0])


def solution(mesh):
    placed = (
        P("ctx", "tp"),
        P("ctx", "tp"),
        P("ctx", "tp"),
        P(None, "tp"),
        P("tp"),
        P("ctx", "tp"),
    )
    return jax.shard_map(
        on_device,
        mesh=mesh,
        in_specs=placed,
        out_specs=(
            P("ctx", "tp"),
            P("ctx", "tp"),
            P("ctx", "tp"),
            P("ctx", "tp"),
            P(None, "tp"),
            P("tp"),
        ),
        check_vma=False,
    )
```
